1024 devices in a mesh: dp: 4 (over y), expert: 32 (over z_hi, x, core), tensor: 8 (over z_lo).
Axes of the slice: x: 4, y: 4, z: 32 (z_hi: 4, z_lo: 8; z = z_hi * 8 + z_lo), core: 2. Of those that a mesh axis runs over, the one named last changes fastest.
Arguments:
- tokens: bfloat16 [1536, 4096], P(('dp', 'expert'), 'tensor'), may hold values from -60 to 60
- grad_out: bfloat16 [1536, 4096], P(('dp', 'expert'), 'tensor'), may hold values from -6 to 6
- route_ids: int32 [1536, 8], P(('dp', 'expert')), may hold values from 0 to 31, all different within a row; in each aligned block of 12 rows (0 to 11, 12 to 23, ...) at most 4 rows name the same one
- route_probs: float32 [1536, 8], P(('dp', 'expert')), may hold values from 0.05 to 1
- w_gate: bfloat16 [32, 4096, 1536], P('expert', None, 'tensor'), may hold values from -0.09375 to 0.09375
- w_up: bfloat16 [32, 4096, 1536], P('expert', None, 'tensor'), may hold values from -0.09375 to 0.09375
- w_down: bfloat16 [32, 1536, 4096], P('expert', 'tensor'), may hold values from -0.15625 to 0.15625
Outputs:
- mixed: bfloat16 [1536, 4096], P(('dp', 'expert'), 'tensor')
- grad_tokens: bfloat16 [1536, 4096], P(('dp', 'expert'), 'tensor')
- grad_down: float32 [32, 1536, 4096], P('expert', 'tensor', 'dp')
The draws below stay inside these ranges and needn't reach their ends.
Inputs may be any that keep to these rules, and one draw needn't show every extreme that they name: `route_ids`: each row names 8 different experts; in the rows of one device (aligned blocks of 12 rows) no expert is named more than 4 times, a bound that some block reaches.
All inputs are finite; a program needn't handle non-finite values. Where the reference program divides by a largest or mean magnitude, that divisor is 1e-20 or more.
Results may differ from the reference program's by a relative error of at most 0.015.
Values may be sent and summed in bfloat16 or wider, within the bound.
A program may use at most 64 MiB of HBM per device.

```python
import math
import jax
import jax.numpy as jnp
import numpy as np
from jax import lax

D = 4096
FF = 1536
EXPERTS = 32
TOPK = 8
TOK_DEV = 12
CAP = 4
HID_PART = 192
TOKENS = 1536
N_DP = 4


def draw_tokens(key, part):
    first_key = jax.random.fold_in(jax.random.fold_in(key, 17), 0)
    columns = jnp.arange(D, dtype=jnp.float32) / (D - 1)
    base = jnp.clip(jax.random.normal(first_key, (TOKENS, D), jnp.float32), -6.0, 6.0)
    values = base * jnp.exp(columns * jnp.log(3.0))[None, :]
    return values.astype(jnp.bfloat16)


def block_levels(key, shape, cuts, low, high):
    def one(dim, shards_of):
        heights = jax.random.uniform(jax.random.fold_in(jax.random.fold_in(key, 6), dim), (shards_of,), jnp.float32, low / len(cuts), high / len(cuts))
        return jnp.repeat(jnp.exp(heights), shape[dim] // shards_of).reshape((-1,) + (1,) * (len(shape) - dim - 1))

    loudness = one(*cuts[0])
    for cut in cuts[1:]:
        loudness = loudness * one(*cut)
    return loudness


def deal_out(own_key, own, number, rows, amount, top, reach, skew):
    sequence = jax.random.permutation(own_key, amount)
    heavy_load, common = shares(amount, rows * top, reach, skew, True), shares(amount, rows * top, reach, skew, False)
    places = jnp.arange(amount)

    def named(tallies, turn):
        used = int((tallies > 0).sum())
        fixed = max(1, used // 4)
        shifted = fixed + (places - fixed + turn * (used - fixed)) % max(1, amount - fixed)
        return jnp.zeros((amount,), jnp.int32).at[sequence[jnp.where(places < fixed, places, shifted)]].set(jnp.asarray(tallies, jnp.int32))

    tallies = jnp.where(number % 4 == 0, named(heavy_load, number // 4), named(common, number - number // 4 - 1))
    mixed = jax.random.permutation(jax.random.fold_in(own, 3), amount)
    source_of, sink = mixed[0:amount // 2 * 2:2], mixed[1:amount // 2 * 2:2]
    slack = jnp.minimum(tallies[source_of] - 1, reach - tallies[sink]) // 2
    slack = jnp.where((source_of == sequence[0]) | (sink == sequence[0]) | (tallies[sink] == 0), 0, jnp.maximum(slack, 0))
    shifted = jax.random.randint(jax.random.fold_in(own, 4), (amount // 2,), 0, 1 << 20) % (slack + 1)
    tallies = tallies.at[source_of].add(-shifted).at[sink].add(shifted)
    members = jnp.searchsorted(jnp.cumsum(tallies), jnp.arange(rows * top), side="right").astype(jnp.int32)
    listing = members.reshape(top, rows).T
    listing = listing[jax.random.permutation(jax.random.fold_in(own, 1), rows)]
    turn = jax.random.randint(jax.random.fold_in(own, 2), (rows, 1), 0, top)
    return jnp.take_along_axis(listing, (jnp.arange(top)[None, :] + turn) % top, axis=1)


def shares(count, total, bound, lean, full):
    weights = [(1 << 20) // math.isqrt(standing ** lean) + 1 for standing in range(1, count + 1)]
    largest = bound if full else min(bound, max(-(-total // count), total * weights[0] // sum(weights)))
    least = 1 if total - largest >= count - 1 else 0
    holding, rest = [largest] + [least] * (count - 1), total - largest - least * (count - 1)
    while rest > 0:
        movable = [i for i in range(1, count) if holding[i] < largest] or [i for i in range(1, count) if holding[i] < bound]
        pool, left = sum([weights[i] for i in movable]), rest
        for i in movable:
            extra = min(bound - holding[i], max(1, left * weights[i] // pool), rest)
            holding[i] = holding[i] + extra
            rest = rest - extra
    return np.array(holding)


def normal_values(rng, shape, deviation, most, pieces=(), kind=jnp.bfloat16):
    level = block_levels(rng, shape, pieces, -0.22, 0.18) if pieces else 1.0
    entries = jax.random.normal(rng, shape, jnp.float32) * deviation * level
    return jnp.minimum(jnp.maximum(entries, -most), most).astype(kind)


def setup_inputs(seed: int = 0) -> dict:
    streams_of = jax.random.split(jax.random.key(seed), 8)
    tokens = draw_tokens(jax.random.fold_in(streams_of[7], 71), 0)
    grad_out = normal_values(streams_of[1], (TOKENS, D), 1.0, 6.0, ((0, 128), (1, 8)))
    route_ids_keys = jax.random.split(jax.random.fold_in(streams_of[2], 1), TOKENS // TOK_DEV)
    route_ids_turns = jax.random.permutation(jax.random.fold_in(streams_of[2], 3), TOKENS // TOK_DEV)
    route_ids = jax.vmap(lambda own, number: deal_out(jax.random.fold_in(streams_of[2], 2), own, number, TOK_DEV, EXPERTS, TOPK, CAP, 2))(route_ids_keys, route_ids_turns).reshape((TOKENS, TOPK))
    route_probs = jnp.clip(0.05 + 0.95 * jax.random.uniform(streams_of[3], (TOKENS, TOPK), jnp.float32) ** block_levels(streams_of[3], (TOKENS, TOPK), ((0, 128),), -0.2, 0.2), 0.05, 1.0)
    w_gate = normal_values(streams_of[4], (EXPERTS, D, FF), D ** -0.5, 0.09375, ((0, 32), (2, 8)))
    w_up = normal_values(streams_of[5], (EXPERTS, D, FF), D ** -0.5, 0.09375, ((0, 32), (2, 8)))
    w_down = normal_values(streams_of[6], (EXPERTS, FF, D), FF ** -0.5, 0.15625, ((0, 32), (1, 8)))
    return dict(tokens=tokens, grad_out=grad_out, route_ids=route_ids, route_probs=route_probs, w_gate=w_gate, w_up=w_up, w_down=w_down)


def pair_slots(block_ids):
    flat_ids = block_ids.reshape(-1).astype(jnp.int32)
    onehot = (flat_ids[:, None] == jnp.arange(EXPERTS, dtype=jnp.int32)[None, :]).astype(jnp.int32)
    slot_rank = jnp.sum(onehot * (jnp.cumsum(onehot, axis=0) - 1), axis=1)
    return (flat_ids * CAP + slot_rank).astype(jnp.int32)


def slot_owner(pair_slot):
    count = pair_slot.shape[0]
    owner = jnp.zeros((EXPERTS * CAP,), jnp.int32).at[pair_slot].set(jnp.arange(count, dtype=jnp.int32))
    live = jnp.zeros((EXPERTS * CAP,), jnp.float32).at[pair_slot].set(jnp.ones((count,), jnp.float32))
    return owner, live


def reference(tokens, grad_out, route_ids, route_probs, w_gate, w_up, w_down):
    blocks = TOKENS // TOK_DEV
    per_block = TOK_DEV * TOPK
    rows_per = blocks * CAP
    parts = FF // HID_PART
    pair_slot = jax.vmap(pair_slots)(route_ids.reshape(blocks, TOK_DEV, TOPK))
    owner, live = jax.vmap(slot_owner)(pair_slot)
    owner = owner + (jnp.arange(blocks, dtype=jnp.int32) * per_block)[:, None]
    owner = owner.reshape(blocks, EXPERTS, CAP).transpose(1, 0, 2).reshape(EXPERTS, rows_per)
    live = live.reshape(blocks, EXPERTS, CAP).transpose(1, 0, 2).reshape(EXPERTS, rows_per)
    magnitude = jnp.max(jnp.abs(tokens.astype(jnp.float32)), axis=1)
    factor = 4.0 / (magnitude + 1e-5)
    scaled = (tokens.astype(jnp.float32) * factor[:, None]).astype(jnp.bfloat16)
    pair_grad = (route_probs[:, :, None] * grad_out.astype(jnp.float32)[:, None, :]).astype(jnp.bfloat16)
    pair_grad = pair_grad.reshape(TOKENS * TOPK, D)

    def expert_pass(items):
        rows_pair, rows_live, gate_w, up_w, down_w = items
        keep = rows_live[:, None] > 0
        token_rows = (rows_pair // TOPK).astype(jnp.int32)
        x_rows = jnp.where(keep, scaled[token_rows], jnp.zeros((), scaled.dtype))
        g_rows = jnp.where(keep, pair_grad[rows_pair], jnp.zeros((), pair_grad.dtype))
        row_factor = factor[token_rows] * rows_live
        gate = jnp.dot(x_rows, gate_w, preferred_element_type=jnp.float32)
        upval = jnp.dot(x_rows, up_w, preferred_element_type=jnp.float32)
        sigma = jax.nn.sigmoid(gate)
        active = gate * sigma
        hidden = (active * upval).astype(jnp.bfloat16)
        hid_split = hidden.astype(jnp.float32).reshape(-1, parts, HID_PART)
        down_split = down_w.astype(jnp.float32).reshape(parts, HID_PART, D)
        out_pieces = jnp.einsum("rtf,tfd->rtd", hid_split, down_split).astype(jnp.bfloat16)
        expert_out = jnp.sum(lax.optimization_barrier(out_pieces).astype(jnp.float32), axis=1).astype(jnp.bfloat16)
        grad_hidden = jnp.dot(g_rows, down_w.T, preferred_element_type=jnp.float32)
        grad_gate = (grad_hidden * upval * sigma * (1.0 + gate * (1.0 - sigma))).astype(jnp.bfloat16)
        grad_up = (grad_hidden * active).astype(jnp.bfloat16)
        gate_split = gate_w.astype(jnp.float32).reshape(D, parts, HID_PART)
        up_split = up_w.astype(jnp.float32).reshape(D, parts, HID_PART)
        dx_pieces = jnp.einsum("rtf,dtf->rtd", grad_gate.astype(jnp.float32).reshape(-1, parts, HID_PART), gate_split)
        dx_pieces = dx_pieces + jnp.einsum("rtf,dtf->rtd", grad_up.astype(jnp.float32).reshape(-1, parts, HID_PART), up_split)
        dx_pieces = (dx_pieces * row_factor[:, None, None]).astype(jnp.bfloat16)
        pair_dx = jnp.sum(lax.optimization_barrier(dx_pieces).astype(jnp.float32), axis=1).astype(jnp.bfloat16)
        hid_groups = hidden.astype(jnp.float32).reshape(N_DP, -1, FF)
        grad_groups = g_rows.astype(jnp.float32).reshape(N_DP, -1, D)
        grad_terms = jnp.einsum("prf,prd->pfd", hid_groups, grad_groups).astype(jnp.bfloat16)
        grad_down = jnp.sum(lax.optimization_barrier(grad_terms).astype(jnp.float32), axis=0)
        return expert_out, pair_dx, grad_down

    expert_out, pair_dx, grad_down = lax.map(expert_pass, (owner, live, w_gate, w_up, w_down))
    block_base = (jnp.arange(blocks, dtype=jnp.int32) * CAP)[:, None]
    flat_index = ((pair_slot // CAP) * rows_per + block_base + pair_slot % CAP).astype(jnp.int32)
    flat_index = flat_index.reshape(TOKENS, TOPK)
    gathered_out = expert_out.reshape(EXPERTS * rows_per, D)[flat_index].astype(jnp.float32)
    mixed = jnp.sum(gathered_out * route_probs[:, :, None], axis=1).astype(jnp.bfloat16)
    gathered_dx = pair_dx.reshape(EXPERTS * rows_per, D)[flat_index].astype(jnp.float32)
    grad_tokens = jnp.sum(gathered_dx, axis=1).astype(jnp.bfloat16)
    return mixed, grad_tokens, grad_down
```

```python
import jax
import jax.numpy as jnp
from jax import lax
from jax.sharding import PartitionSpec as P

EXPERTS = 32
amax_target = 4.0
eps_scale = 1e-05
PLANE = ("expert", "tensor")
bf16, f32 = jnp.bfloat16, jnp.float32


def on_device(tokens, grad_out, route_ids, route_probs, w_gate, w_up, w_down):
    rows, width = tokens.shape
    n_e, n_t = lax.axis_size("expert"), lax.axis_size("tensor")
    me = lax.axis_index("expert")
    both = jnp.stack([tokens, grad_out])
    whole = lax.all_gather(both, PLANE, axis=0, tiled=False)
    whole = whole.reshape(n_e, n_t, 2, rows, width).transpose(2, 0, 3, 1, 4)
    whole = whole.reshape(2, n_e * rows, n_t * width)
    x, g = whole[0], whole[1]
    dense = jnp.sum(
        jnp.where(
            route_ids[:, :, None] == jnp.arange(EXPERTS, dtype=jnp.int32), route_probs[:, :, None], 0.0
        ),
        axis=1,
    )
    probs = lax.all_gather(dense, "expert", axis=0, tiled=True)
    prob = lax.dynamic_slice_in_dim(probs, me, 1, axis=1)
    live = prob > 0
    magnitude = jnp.max(jnp.abs(x), axis=1, keepdims=True).astype(f32)
    factor = amax_target / (magnitude + eps_scale)
    wg, wu, wd = w_gate[0], w_up[0], w_down[0]
    gate = factor * jnp.dot(x, wg, preferred_element_type=f32)
    upval = factor * jnp.dot(x, wu, preferred_element_type=f32)
    sigma = jax.nn.sigmoid(gate)
    active = gate * sigma
    hidden = (jnp.where(live, prob, 0.0) * active * upval).astype(bf16)
    gh = jnp.einsum("rd,fd->rf", g, wd, preferred_element_type=f32) * (prob * factor)
    gg = (gh * upval * sigma * (1.0 + gate * (1.0 - sigma))).astype(bf16)
    gu = (gh * active).astype(bf16)
    dx = jnp.einsum("rf,df->rd", gg, wg, preferred_element_type=f32)
    dx = dx + jnp.einsum("rf,df->rd", gu, wu, preferred_element_type=f32)
    out = jnp.dot(hidden, wd, preferred_element_type=f32)
    parts = jnp.stack([out.astype(bf16), dx.astype(bf16)])
    parts = parts.reshape(2, n_e, rows, n_t, width).transpose(1, 3, 0, 2, 4)
    parts = parts.reshape(n_e * n_t, 2 * rows, width)
    mine = lax.psum_scatter(parts, PLANE, scatter_dimension=0, tiled=False)
    mixed, grad_tokens = mine[:rows], mine[rows:]
    term = jnp.einsum("rf,rd->fd", hidden, g, preferred_element_type=f32).astype(bf16)
    n_dp = lax.axis_size("dp")
    pieces = jnp.moveaxis(term.reshape(term.shape[0], n_dp, -1), 1, 0)
    pieces = lax.all_to_all(pieces, "dp", 0, 0, tiled=True)
    grad_down = jnp.sum(pieces.astype(f32), axis=0)[None]
    return (mixed, grad_tokens, grad_down)


def solution(mesh):
    return jax.shard_map(
        on_device,
        mesh=mesh,
        in_specs=(
            P(("dp", "expert"), "tensor"),
            P(("dp", "expert"), "tensor"),
            P(("dp", "expert"), None),
            P(("dp", "expert"), None),
            P("expert", None, "tensor"),
            P("expert", None, "tensor"),
            P("expert", "tensor", None),
        ),
        out_specs=(
            P(("dp", "expert"), "tensor"),
            P(("dp", "expert"), "tensor"),
            P("expert", "tensor", "dp"),
        ),
        check_vma=False,
    )
```

```python
import functools

import jax
import jax.numpy as jnp
import numpy as np
from jax import lax
from jax.experimental import pallas as pl
from jax.experimental.pallas import tpu as pltpu
from jax.sharding import PartitionSpec as P

EXPERTS = 32
AMAX_TARGET = 4.0
EPS_SCALE = 1e-05
LANES = 128
NX, NC = 4, 2
P_ROWS = 16
bf16, f32 = jnp.bfloat16, jnp.float32
MESH = pl.DeviceIdType.MESH
VMEM_BYTES = 56 * 1024 * 1024


def mm(a, b):
    return jnp.dot(a, b, preferred_element_type=f32)


def mm_nt(a, b):
    return lax.dot_general(a, b, (((1,), (1,)), ((), ())), preferred_element_type=f32)


def mm_tn(a, b):
    return lax.dot_general(a, b, (((0,), (0,)), ((), ())), preferred_element_type=f32)


def kernel(
    ny, nh, nz, tok, wid,
    blk, perm, permt, permp, wg_h, wu_h, wd_h,
    out, gd,
    hbuf, pb, xb, wg, wu, wd, gate_acc, up_acc, gh_acc, amax, hp, gg, gu,
    cb, sb, xr1, xl1, xr2, xl2, zs, zr, zl_buf, wt, yr1, yl1, yr2, yl2, fp, hb2,
    w_sem, h_s, h_r, p_s, p_r, z_s, z_r, xa_s, xa_r, xb_s, xb_r, sib_s, sib_r,
    cs_s, cs_r, x1_s, x1_r, x2_s, x2_r, zz_s, zz_r, y_s, y_r, f_s, f_r,
):
    half = nz // 2
    q_n = wid // LANES
    rows = nh * tok
    every = NX * NC * rows
    packed = q_n * tok
    y, e, z = lax.axis_index("dp"), lax.axis_index("expert"), lax.axis_index("tensor")
    c = lax.rem(e, NC)
    x = lax.rem(e // NC, NX)
    h = e // (NC * NX)

    def eid(h_, x_, c_):
        return (h_ * NX + x_) * NC + c_

    x_right, x_left, x_far = (lax.rem(x + k, NX) for k in (1, 3, 2))
    d_xr, d_xl, d_xf = ((y, eid(h, k, c), z) for k in (x_right, x_left, x_far))
    d_sib = (y, eid(h, x, 1 - c), z)
    d_zr = (y, eid(lax.rem(h + (z + 1) // nz, nh), x, c), lax.rem(z + 1, nz))
    d_zl = (
        y,
        eid(lax.rem(h + nh - 1 + (z + nz - 1) // nz, nh), x, c),
        lax.rem(z + nz - 1, nz),
    )
    d_h = [(y, eid(lax.rem(h + k, nh), x, c), z) for k in range(1, nh)]
    d_yr, d_yl = (lax.rem(y + 1, ny), e, z), (lax.rem(y + ny - 1, ny), e, z)

    def rdma(src, dst, s, r, dev):
        return pltpu.make_async_remote_copy(
            src_ref=src, dst_ref=dst, send_sem=s, recv_sem=r, device_id=dev, device_id_type=MESH
        )

    loads = [
        pltpu.make_async_copy(a, b, w_sem.at[i])
        for i, (a, b) in enumerate(((wg_h, wg), (wu_h, wu), (wd_h, wd)))
    ]
    for load in loads:
        load.start()

    partners = [d_xr, d_xl, d_xf, d_sib, d_zr, d_zl, *d_h]
    if ny > 1:
        partners += [d_yr, d_yl]
    barrier = pltpu.get_barrier_semaphore()
    for dev in partners:
        pl.semaphore_signal(barrier, inc=1, device_id=dev, device_id_type=MESH)
    pl.semaphore_wait(barrier, len(partners))

    h_out = [
        rdma(blk, hbuf.at[h], h_s.at[k], h_r.at[k], dev) for k, dev in enumerate(d_h)
    ]
    for cp in h_out:
        cp.start()
    hbuf[pl.ds(h, 1)] = blk[...][None]
    gate_acc[...] = jnp.zeros_like(gate_acc)
    up_acc[...] = jnp.zeros_like(up_acc)
    gh_acc[...] = jnp.zeros_like(gh_acc)
    amax[...] = jnp.zeros_like(amax)
    zr[0, 1] = jnp.zeros_like(zr[0, 1])
    zl_buf[0, 0] = jnp.zeros_like(zl_buf[0, 0])
    for cp in h_out:
        cp.wait_recv()
    for a in range(2):
        block = hbuf[:, a * packed : (a + 1) * packed, :].reshape(nh * packed, LANES)
        spread = mm(perm[...], block).astype(bf16)
        for q in range(q_n):
            xb[z, a, x, c, :, q * LANES : (q + 1) * LANES] = spread[q * rows : (q + 1) * rows]
    pieces = hbuf[:, 2 * packed :, :].reshape(nh * P_ROWS, LANES)
    pb[x, c] = mm(permp[...], pieces).astype(bf16)

    def at_step(t):
        d = (t + 1) // 2
        return lax.rem(z + d * (1 - 2 * lax.rem(t, 2)) + nz, nz)

    def z_copy(way, d, split):
        s = lax.rem(z + (d if way else -d) + nz, nz)
        ref = xb.at[s, way, x, c] if split else xb.at[s, :, x, c]
        return rdma(ref, ref, z_s.at[way, d], z_r.at[way, d], d_zl if way else d_zr)

    def z_send(way, d):
        @pl.when(d < half - 1)
        def _():
            z_copy(way, d, False).start()

        @pl.when(d == half - 1)
        def _():
            z_copy(way, d, True).start()

    def xa_copy(t, way):
        ref = xb.at[at_step(t), :, x, c]
        return rdma(ref, ref, xa_s.at[way, t], xa_r.at[way, t], d_xl if way else d_xr)

    def xb_copy(t, way):
        ref = xb.at[at_step(t), way, x_right if way else x_left, c]
        return rdma(ref, ref, xb_s.at[way, t], xb_r.at[way, t], d_xl if way else d_xr)

    def sib_copy(t):
        ref = xb.at[at_step(t), :, :, c]
        return rdma(ref, ref, sib_s.at[t], sib_r.at[t], d_sib)

    def p_copy(k):
        ref = pb.at[x, c]
        return rdma(ref, ref, p_s.at[k], p_r.at[k], (d_xr, d_xl, d_xf)[k])

    def p_sib():
        ref = pb.at[:, c]
        return rdma(ref, ref, p_s.at[3], p_r.at[3], d_sib)

    def gather_step(t, carry):
        @pl.when(t < nz)
        def _():
            d = (t + 1) // 2
            odd = lax.rem(t, 2)

            @pl.when(t == 0)
            def _():
                z_send(0, t)
                z_send(1, t)

            @pl.when((odd == 1) & (t < nz - 1))
            def _():
                z_copy(0, d - 1, False).wait_recv()
                z_send(0, d)

            @pl.when((odd == 0) & (t > 0))
            def _():
                z_copy(1, d - 1, False).wait_recv()
                z_send(1, d)

            @pl.when(t == nz - 1)
            def _():
                z_copy(0, half - 1, True).wait_recv()
                z_copy(1, half - 1, True).wait_recv()

            for way in range(2):
                xa_copy(t, way).start()

            @pl.when(t == 0)
            def _():
                for k in range(3):
                    p_copy(k).start()

        @pl.when((t >= 1) & (t < nz + 1))
        def _():
            for way in range(2):
                xa_copy(t - 1, way).wait_recv()
                xb_copy(t - 1, way).start()

        @pl.when((t >= 2) & (t < nz + 2))
        def _():
            for way in range(2):
                xb_copy(t - 2, way).wait_recv()
            sib_copy(t - 2).start()

            @pl.when(t == 2)
            def _():
                for k in range(3):
                    p_copy(k).wait_recv()
                p_sib().start()

        @pl.when(t == 3)
        def _():
            for load in loads:
                load.wait()

        @pl.when(t >= 3)
        def _():
            sib_copy(t - 3).wait_recv()
            s = at_step(t - 3)
            cols = pl.ds(pl.multiple_of(s * wid, wid), wid)
            x_rows = xb[s, 0].reshape(every, wid)
            gate_acc[...] += mm(x_rows, wg[cols, :])
            up_acc[...] += mm(x_rows, wu[cols, :])
            gh_acc[...] += mm_nt(xb[s, 1].reshape(every, wid), wd[:, cols])
            size = jnp.abs(x_rows.astype(f32))
            top = amax[...]
            for q in range(q_n):
                top = jnp.maximum(top, size[:, q * LANES : (q + 1) * LANES])
            amax[...] = top

        return carry

    lax.fori_loop(0, nz + 3, gather_step, 0)

    p_sib().wait_recv()
    lane = lax.broadcasted_iota(jnp.int32, (every, LANES), 1)
    mine = (lane == e) | (lane == e + EXPERTS) | (lane == e + 2 * EXPERTS)
    prob = jnp.sum(
        jnp.where(mine, pb[...].reshape(every, LANES).astype(f32), 0.0), axis=1, keepdims=True
    )
    factor = AMAX_TARGET / (jnp.max(amax[...], axis=1, keepdims=True) + EPS_SCALE)
    gate = gate_acc[...] * factor
    upval = up_acc[...] * factor
    sigma = jax.nn.sigmoid(gate)
    active = gate * sigma
    grad = gh_acc[...] * (prob * factor)
    hp[...] = (prob * active * upval).astype(bf16)
    gg[...] = (grad * upval * sigma * (1.0 + gate * (1.0 - sigma))).astype(bf16)
    gu[...] = (grad * active).astype(bf16)

    def y_term(dest):
        for k in range(2):
            wt[dest, k] = mm_tn(hp[...], xb[2 * dest + k, 1].reshape(every, wid)).astype(bf16)

    y_far, y_right, y_left = (lax.rem(y + k, ny) for k in (2, 1, 3))

    def y1_copy(way):
        src, dst = wt.at[y_far, way], (yl1 if way else yr1)
        return rdma(src, dst, y_s.at[way], y_r.at[way], d_yl if way else d_yr)

    def y2_copy(way):
        src, dst = wt.at[y_left if way else y_right], (yl2 if way else yr2)
        return rdma(src, dst, y_s.at[2 + way], y_r.at[2 + way], d_yl if way else d_yr)

    def dest_of(k):
        odd = lax.rem(k, 2)
        off = jnp.where(odd == 1, half - (k + 1) // 2, k // 2 - half)
        return lax.rem(z + off + nz, nz)

    def cs_copy(k):
        return rdma(cb.at[k, :, :, 1 - c], sb.at[k], cs_s.at[k], cs_r.at[k], d_sib)

    def x1_copy(k, way):
        dst = (xl1 if way else xr1).at[k]
        return rdma(cb.at[k, way, x_far, c], dst, x1_s.at[way, k], x1_r.at[way, k], d_xl if way else d_xr)

    def x2_copy(k, way):
        src = cb.at[k, :, x_left if way else x_right, c]
        dst = (xl2 if way else xr2).at[k]
        return rdma(src, dst, x2_s.at[way, k], x2_r.at[way, k], d_xl if way else d_xr)

    def zz_copy(way, m, first):
        k = 2 * m if way else jnp.maximum(2 * m - 1, 0)
        src, dst = zs.at[k], (zl_buf if way else zr).at[m]
        if first:
            src, dst = src.at[way], dst.at[way]
        return rdma(src, dst, zz_s.at[way, m], zz_r.at[way, m], d_zl if way else d_zr)

    def zz_wait(way, m):
        @pl.when(m == 0)
        def _():
            zz_copy(way, m, True).wait_recv()

        @pl.when(m > 0)
        def _():
            zz_copy(way, m, False).wait_recv()

    def sum_step(t, carry):
        @pl.when(t < nz)
        def _():
            s = dest_of(t)
            cols = pl.ds(pl.multiple_of(s * wid, wid), wid)
            o = mm(hp[...], wd[:, cols])
            cb[t, 0] = o.astype(bf16).reshape(NX, NC, rows, wid)
            dx = mm_nt(gg[...], wg[cols, :]) + mm_nt(gu[...], wu[cols, :])
            cb[t, 1] = dx.astype(bf16).reshape(NX, NC, rows, wid)
            cs_copy(t).start()

        if ny > 1:

            @pl.when(t == 0)
            def _():
                y_term(y_far)
                for way in range(2):
                    y1_copy(way).start()

        @pl.when((t >= 1) & (t < nz + 1))
        def _():
            k = t - 1
            cs_copy(k).wait_recv()
            cb[k, :, :, c] = (cb[k, :, :, c].astype(f32) + sb[k].astype(f32)).astype(bf16)
            for way in range(2):
                x1_copy(k, way).start()

        if ny > 1:

            @pl.when(t == 1)
            def _():
                y_term(y_right)
                y_term(y_left)

        @pl.when((t >= 2) & (t < nz + 2))
        def _():
            k = t - 2
            for way in range(2):
                x1_copy(k, way).wait_recv()
                to = x_left if way else x_right
                came = (xl1 if way else xr1)[k]
                cb[k, way, to, c] = (cb[k, way, to, c].astype(f32) + came.astype(f32)).astype(bf16)
                x2_copy(k, way).start()

        if ny > 1:

            @pl.when(t == min(4, nz + 2))
            def _():
                for way in range(2):
                    y1_copy(way).wait_recv()
                    to = y_left if way else y_right
                    came = (yl1 if way else yr1)[...]
                    wt[to, way] = (wt[to, way].astype(f32) + came.astype(f32)).astype(bf16)
                    y2_copy(way).start()
                y_term(y)

        @pl.when(t >= 3)
        def _():
            k = t - 3
            for way in range(2):
                x2_copy(k, way).wait_recv()
            got = cb[k, :, x, c].astype(f32) + xr2[k].astype(f32) + xl2[k].astype(f32)
            odd = lax.rem(k, 2)

            @pl.when(k == 0)
            def _():
                zs[0] = got.astype(bf16)
                for way in range(2):
                    zz_copy(way, 0, True).start()

            @pl.when((odd == 1) & (k < nz - 1))
            def _():
                m = (k + 1) // 2
                zz_wait(0, m - 1)
                zs[k] = (got + zr[m - 1].astype(f32)).astype(bf16)
                zz_copy(0, m, False).start()

            @pl.when((odd == 0) & (k > 0))
            def _():
                m = k // 2
                zz_wait(1, m - 1)
                zs[k] = (got + zl_buf[m - 1].astype(f32)).astype(bf16)
                zz_copy(1, m, False).start()

            @pl.when(k == nz - 1)
            def _():
                for way in range(2):
                    zz_copy(way, half - 1, half == 1).wait_recv()
                both = zr[half - 1].astype(f32) + zl_buf[half - 1].astype(f32)
                zs[k] = (got + both).astype(bf16)

        return carry

    lax.fori_loop(0, nz + 3, sum_step, 0)

    for a in range(2):
        final = zs[nz - 1, a]
        stacked = jnp.concatenate(
            [final[:, q * LANES : (q + 1) * LANES] for q in range(q_n)], axis=0
        )
        fp[:, a * packed : (a + 1) * packed, :] = (
            mm(permt[...], stacked).astype(bf16).reshape(nh, packed, LANES)
        )
    f_out = [
        rdma(fp.at[lax.rem(h + k + 1, nh)], hb2.at[k], f_s.at[k], f_r.at[k], dev)
        for k, dev in enumerate(d_h)
    ]
    for cp in f_out:
        cp.start()

    if ny > 1:
        for way in range(2):
            y2_copy(way).wait_recv()
        for k in range(2):
            total = wt[y, k].astype(f32) + yr2[k].astype(f32) + yl2[k].astype(f32)
            gd[:, k * wid : (k + 1) * wid] = total
    else:
        y_term(y)
        for k in range(2):
            gd[:, k * wid : (k + 1) * wid] = wt[y, k].astype(f32)

    for cp in f_out:
        cp.wait_recv()
    total = fp[h].astype(f32)
    for k in range(nh - 1):
        total = total + hb2[k].astype(f32)
    out[...] = total.astype(bf16)

    for cp in (*h_out, *f_out):
        cp.wait_send()
    for k in range(3):
        p_copy(k).wait_send()
    p_sib().wait_send()
    if ny > 1:
        for way in range(2):
            y1_copy(way).wait_send()
            y2_copy(way).wait_send()

    def z_drain(d, carry):
        for way in range(2):
            z_copy(way, d, False).wait_send()
        return carry

    def zz_drain(m, carry):
        for way in range(2):
            zz_copy(way, m, False).wait_send()
        return carry

    lax.fori_loop(0, half - 1, z_drain, 0)
    lax.fori_loop(1, half, zz_drain, 0)
    for way in range(2):
        z_copy(way, half - 1, True).wait_send()
        zz_copy(way, 0, True).wait_send()

    def drain(t, carry):
        for way in range(2):
            xa_copy(t, way).wait_send()
            xb_copy(t, way).wait_send()
            x1_copy(t, way).wait_send()
            x2_copy(t, way).wait_send()
        sib_copy(t).wait_send()
        cs_copy(t).wait_send()
        return carry

    lax.fori_loop(0, nz, drain, 0)


def permutations(nh, tok, q_n):
    rows, packed = nh * tok, q_n * tok
    perm = np.zeros((q_n * rows, nh * packed), np.float32)
    permp = np.zeros((rows, nh * P_ROWS), np.float32)
    for h in range(nh):
        for i in range(tok):
            permp[h * tok + i, h * P_ROWS + i] = 1
            for q in range(q_n):
                perm[q * rows + h * tok + i, h * packed + q * tok + i] = 1
    return tuple(jnp.asarray(a, bf16) for a in (perm, perm.T, permp))


def fused(blk, wg, wu, wd, ny, nh, nz, tok):
    width, hid = wg.shape
    wid = width // nz
    q_n = wid // LANES
    rows = nh * tok
    every = NX * NC * rows
    half = nz // 2
    perms = permutations(nh, tok, q_n)
    vmem, dma = pltpu.VMEM, pltpu.SemaphoreType.DMA
    n_blk = 2 * q_n * tok
    scratch = [
        vmem((nh, n_blk + P_ROWS, LANES), bf16),
        vmem((NX, NC, rows, LANES), bf16),
        vmem((nz, 2, NX, NC, rows, wid), bf16),
        vmem((width, hid), bf16),
        vmem((width, hid), bf16),
        vmem((hid, width), bf16),
        vmem((every, hid), f32),
        vmem((every, hid), f32),
        vmem((every, hid), f32),
        vmem((every, LANES), f32),
        vmem((every, hid), bf16),
        vmem((every, hid), bf16),
        vmem((every, hid), bf16),
        vmem((nz, 2, NX, NC, rows, wid), bf16),
        vmem((nz, 2, NX, rows, wid), bf16),
        vmem((nz, rows, wid), bf16),
        vmem((nz, rows, wid), bf16),
        vmem((nz, 2, rows, wid), bf16),
        vmem((nz, 2, rows, wid), bf16),
        vmem((nz, 2, rows, wid), bf16),
        vmem((half, 2, rows, wid), bf16),
        vmem((half, 2, rows, wid), bf16),
        vmem((nz // 2, 2, hid, wid), bf16),
        vmem((hid, wid), bf16),
        vmem((hid, wid), bf16),
        vmem((2, hid, wid), bf16),
        vmem((2, hid, wid), bf16),
        vmem((nh, n_blk, LANES), bf16),
        vmem((max(nh - 1, 1), n_blk, LANES), bf16),
        dma((3,)),
        dma((3,)),
        dma((3,)),
        dma((4,)),
        dma((4,)),
        dma((2, half)),
        dma((2, half)),
        dma((2, nz)),
        dma((2, nz)),
        dma((2, nz)),
        dma((2, nz)),
        dma((nz,)),
        dma((nz,)),
        dma((nz,)),
        dma((nz,)),
        dma((2, nz)),
        dma((2, nz)),
        dma((2, nz)),
        dma((2, nz)),
        dma((2, half)),
        dma((2, half)),
        dma((4,)),
        dma((4,)),
        dma((3,)),
        dma((3,)),
    ]
    in_vmem, anywhere = pl.BlockSpec(memory_space=pltpu.VMEM), pl.BlockSpec(memory_space=pl.ANY)
    return pl.pallas_call(
        functools.partial(kernel, ny, nh, nz, tok, wid),
        out_shape=(
            jax.ShapeDtypeStruct((n_blk, LANES), bf16),
            jax.ShapeDtypeStruct((hid, 2 * wid), f32),
        ),
        in_specs=[in_vmem] * 4 + [anywhere] * 3,
        out_specs=(in_vmem, in_vmem),
        scratch_shapes=scratch,
        compiler_params=pltpu.CompilerParams(
            collective_id=0, has_side_effects=True, vmem_limit_bytes=VMEM_BYTES
        ),
        cost_estimate=pl.CostEstimate(
            flops=14 * every * width * hid, bytes_accessed=6 * width * hid, transcendentals=every * hid
        ),
    )(blk, *perms, wg, wu, wd)


def on_device(tokens, grad_out, route_ids, route_probs, w_gate, w_up, w_down):
    tok, wid = tokens.shape
    q_n = wid // LANES
    ny, nz = lax.axis_size("dp"), lax.axis_size("tensor")
    nh = lax.axis_size("expert") // (NX * NC)

    def pack(a):
        return a.reshape(tok, q_n, LANES).transpose(1, 0, 2).reshape(q_n * tok, LANES)

    def unpack(a):
        return a.reshape(q_n, tok, LANES).transpose(1, 0, 2).reshape(tok, wid)

    named = route_ids[:, :, None] == jnp.arange(EXPERTS, dtype=jnp.int32)
    dense = jnp.sum(jnp.where(named, route_probs[:, :, None], 0.0), axis=1)
    high = lax.reduce_precision(dense, 8, 7)
    middle = lax.reduce_precision(dense - high, 8, 7)
    pieces = jnp.concatenate([high, middle, dense - high - middle], axis=1).astype(bf16)
    pieces = jnp.pad(pieces, ((0, P_ROWS - tok), (0, LANES - 3 * EXPERTS)))
    blk = jnp.concatenate([pack(tokens), pack(grad_out), pieces], axis=0)
    both, grad_down = fused(blk, w_gate[0], w_up[0], w_down[0], ny, nh, nz, tok)
    mixed, grad_tokens = unpack(both[: q_n * tok]), unpack(both[q_n * tok :])
    return (mixed, grad_tokens, grad_down[None])


def solution(mesh):
    return jax.shard_map(
        on_device,
        mesh=mesh,
        in_specs=(
            P(("dp", "expert"), "tensor"),
            P(("dp", "expert"), "tensor"),
            P(("dp", "expert"), None),
            P(("dp", "expert"), None),
            P("expert", None, "tensor"),
            P("expert", None, "tensor"),
            P("expert", "tensor", None),
        ),
        out_specs=(
            P(("dp", "expert"), "tensor"),
            P(("dp", "expert"), "tensor"),
            P("expert", "tensor", "dp"),
        ),
        check_vma=False,
    )
```

```python
import functools

import jax
import jax.numpy as jnp
import numpy as np
from jax import lax
from jax.experimental import pallas as pl
from jax.experimental.pallas import tpu as pltpu
from jax.sharding import PartitionSpec as P

EXPERTS = 32
TOPK = 8
AMAX_TARGET = 4.0
EPS_SCALE = 1e-05
LANES = 128
NX, NC = 4, 2
P_ROWS = 16
bf16, f32 = jnp.bfloat16, jnp.float32
MESH = pl.DeviceIdType.MESH
VMEM_BYTES = 56 * 1024 * 1024


def mm(a, b):
    return jnp.dot(a, b, preferred_element_type=f32)


def mm_nt(a, b):
    return lax.dot_general(a, b, (((1,), (1,)), ((), ())), preferred_element_type=f32)


def mm_tn(a, b):
    return lax.dot_general(a, b, (((0,), (0,)), ((), ())), preferred_element_type=f32)


def kernel(
    ny, nh, nz, tok, wid,
    tok_in, go_in, ids_in, probs_in, perm, permt, permp, spread_p, gather_p, wg_h, wu_h, wd_h,
    out_m, out_g, gd,
    blk, pad_in, hbuf, pb, xb, wg, wu, wd, gate_acc, up_acc, gh_acc, amax, hp, gg, gu,
    cb, sb, xr1, xl1, xr2, xl2, zs, zr, zl_buf, wt, yr1, yl1, yr2, yl2, fp, hb2,
    w_sem, h_s, h_r, p_s, p_r, z_s, z_r, xa_s, xa_r, xb_s, xb_r, sib_s, sib_r,
    cs_s, cs_r, x1_s, x1_r, x2_s, x2_r, zz_s, zz_r, y_s, y_r, f_s, f_r,
):
    half = nz // 2
    q_n = wid // LANES
    rows = nh * tok
    every = NX * NC * rows
    packed = q_n * tok
    y, e, z = lax.axis_index("dp"), lax.axis_index("expert"), lax.axis_index("tensor")
    c = lax.rem(e, NC)
    x = lax.rem(e // NC, NX)
    h = e // (NC * NX)

    def eid(h_, x_, c_):
        return (h_ * NX + x_) * NC + c_

    x_right, x_left, x_far = (lax.rem(x + k, NX) for k in (1, 3, 2))
    d_xr, d_xl, d_xf = ((y, eid(h, k, c), z) for k in (x_right, x_left, x_far))
    d_sib = (y, eid(h, x, 1 - c), z)
    d_zr = (y, eid(lax.rem(h + (z + 1) // nz, nh), x, c), lax.rem(z + 1, nz))
    d_zl = (
        y,
        eid(lax.rem(h + nh - 1 + (z + nz - 1) // nz, nh), x, c),
        lax.rem(z + nz - 1, nz),
    )
    d_h = [(y, eid(lax.rem(h + k, nh), x, c), z) for k in range(1, nh)]
    d_yr, d_yl = (lax.rem(y + 1, ny), e, z), (lax.rem(y + ny - 1, ny), e, z)

    def rdma(src, dst, s, r, dev):
        return pltpu.make_async_remote_copy(
            src_ref=src, dst_ref=dst, send_sem=s, recv_sem=r, device_id=dev, device_id_type=MESH
        )

    loads = [
        pltpu.make_async_copy(a, b, w_sem.at[i])
        for i, (a, b) in enumerate(((wg_h, wg), (wu_h, wu), (wd_h, wd)))
    ]
    for load in loads:
        load.start()

    partners = [d_xr, d_xl, d_xf, d_sib, d_zr, d_zl, *d_h]
    if ny > 1:
        partners += [d_yr, d_yl]
    barrier = pltpu.get_barrier_semaphore()
    for dev in partners:
        pl.semaphore_signal(barrier, inc=1, device_id=dev, device_id_type=MESH)

    pad_in[...] = jnp.zeros_like(pad_in)
    for a, ref in enumerate((tok_in, go_in)):
        pad_in[:tok, :] = ref[...]
        tall = jnp.concatenate([pad_in[:, q * LANES : (q + 1) * LANES] for q in range(q_n)], axis=0)
        blk[a * packed : (a + 1) * packed, :] = mm(gather_p[...], tall).astype(bf16)
    expert = lax.broadcasted_iota(jnp.int32, (EXPERTS, LANES), 0)
    dense = jnp.zeros((EXPERTS, LANES), f32)
    for k in range(TOPK):
        dense = dense + jnp.where(expert == ids_in[k : k + 1, :], probs_in[k : k + 1, :], 0.0)
    high = dense.astype(bf16).astype(f32)
    middle = (dense - high).astype(bf16).astype(f32)
    tall = jnp.concatenate([high, middle, dense - high - middle, jnp.zeros_like(dense)], axis=0)
    blk[2 * packed :, :] = tall.T[:P_ROWS].astype(bf16)

    hbuf[pl.ds(h, 1)] = blk[...][None]
    gate_acc[...] = jnp.zeros_like(gate_acc)
    up_acc[...] = jnp.zeros_like(up_acc)
    gh_acc[...] = jnp.zeros_like(gh_acc)
    amax[...] = jnp.zeros_like(amax)
    zr[0, 1] = jnp.zeros_like(zr[0, 1])
    zl_buf[0, 0] = jnp.zeros_like(zl_buf[0, 0])
    pl.semaphore_wait(barrier, len(partners))

    h_out = [
        rdma(blk, hbuf.at[h], h_s.at[k], h_r.at[k], dev) for k, dev in enumerate(d_h)
    ]
    for cp in h_out:
        cp.start()
    for cp in h_out:
        cp.wait_recv()
    for a in range(2):
        block = hbuf[:, a * packed : (a + 1) * packed, :].reshape(nh * packed, LANES)
        spread = mm(perm[...], block).astype(bf16)
        for q in range(q_n):
            xb[z, a, x, c, :, q * LANES : (q + 1) * LANES] = spread[q * rows : (q + 1) * rows]
    pieces = hbuf[:, 2 * packed :, :].reshape(nh * P_ROWS, LANES)
    pb[x, c] = mm(permp[...], pieces).astype(bf16)

    def at_step(t):
        d = (t + 1) // 2
        return lax.rem(z + d * (1 - 2 * lax.rem(t, 2)) + nz, nz)

    def z_copy(way, d, split):
        s = lax.rem(z + (d if way else -d) + nz, nz)
        ref = xb.at[s, way, x, c] if split else xb.at[s, :, x, c]
        return rdma(ref, ref, z_s.at[way, d], z_r.at[way, d], d_zl if way else d_zr)

    def z_send(way, d):
        @pl.when(d < half - 1)
        def _():
            z_copy(way, d, False).start()

        @pl.when(d == half - 1)
        def _():
            z_copy(way, d, True).start()

    def xa_copy(t, way):
        ref = xb.at[at_step(t), :, x, c]
        return rdma(ref, ref, xa_s.at[way, t], xa_r.at[way, t], d_xl if way else d_xr)

    def xb_copy(t, way):
        ref = xb.at[at_step(t), way, x_right if way else x_left, c]
        return rdma(ref, ref, xb_s.at[way, t], xb_r.at[way, t], d_xl if way else d_xr)

    def sib_copy(t):
        ref = xb.at[at_step(t), :, :, c]
        return rdma(ref, ref, sib_s.at[t], sib_r.at[t], d_sib)

    def p_copy(k):
        ref = pb.at[x, c]
        return rdma(ref, ref, p_s.at[k], p_r.at[k], (d_xr, d_xl, d_xf)[k])

    def p_sib():
        ref = pb.at[:, c]
        return rdma(ref, ref, p_s.at[3], p_r.at[3], d_sib)

    def gather_step(t, carry):
        @pl.when(t < nz)
        def _():
            d = (t + 1) // 2
            odd = lax.rem(t, 2)

            @pl.when(t == 0)
            def _():
                z_send(0, t)
                z_send(1, t)

            @pl.when((odd == 1) & (t < nz - 1))
            def _():
                z_copy(0, d - 1, False).wait_recv()
                z_send(0, d)

            @pl.when((odd == 0) & (t > 0))
            def _():
                z_copy(1, d - 1, False).wait_recv()
                z_send(1, d)

            @pl.when(t == nz - 1)
            def _():
                z_copy(0, half - 1, True).wait_recv()
                z_copy(1, half - 1, True).wait_recv()

            for way in range(2):
                xa_copy(t, way).start()

            @pl.when(t == 0)
            def _():
                for k in range(3):
                    p_copy(k).start()

        @pl.when((t >= 1) & (t < nz + 1))
        def _():
            for way in range(2):
                xa_copy(t - 1, way).wait_recv()
                xb_copy(t - 1, way).start()

        @pl.when((t >= 2) & (t < nz + 2))
        def _():
            for way in range(2):
                xb_copy(t - 2, way).wait_recv()
            sib_copy(t - 2).start()

            @pl.when(t == 2)
            def _():
                for k in range(3):
                    p_copy(k).wait_recv()
                p_sib().start()

        @pl.when(t == 3)
        def _():
            for load in loads:
                load.wait()

        @pl.when(t >= 3)
        def _():
            sib_copy(t - 3).wait_recv()
            s = at_step(t - 3)
            cols = pl.ds(pl.multiple_of(s * wid, wid), wid)
            x_rows = xb[s, 0].reshape(every, wid)
            gate_acc[...] += mm_nt(x_rows, wg[:, cols])
            up_acc[...] += mm_nt(x_rows, wu[:, cols])
            gh_acc[...] += mm_nt(xb[s, 1].reshape(every, wid), wd[:, cols])
            size = jnp.abs(x_rows.astype(f32))
            top = amax[...]
            for q in range(q_n):
                top = jnp.maximum(top, size[:, q * LANES : (q + 1) * LANES])
            amax[...] = top

        return carry

    lax.fori_loop(0, nz + 3, gather_step, 0)

    p_sib().wait_recv()
    lane = lax.broadcasted_iota(jnp.int32, (every, LANES), 1)
    mine = (lane == e) | (lane == e + EXPERTS) | (lane == e + 2 * EXPERTS)
    prob = jnp.sum(
        jnp.where(mine, pb[...].reshape(every, LANES).astype(f32), 0.0), axis=1, keepdims=True
    )
    factor = AMAX_TARGET / (jnp.max(amax[...], axis=1, keepdims=True) + EPS_SCALE)
    gate = gate_acc[...] * factor
    upval = up_acc[...] * factor
    sigma = jax.nn.sigmoid(gate)
    active = gate * sigma
    grad = gh_acc[...] * (prob * factor)
    hp[...] = (prob * active * upval).astype(bf16)
    gg[...] = (grad * upval * sigma * (1.0 + gate * (1.0 - sigma))).astype(bf16)
    gu[...] = (grad * active).astype(bf16)

    def y_term(dest):
        for k in range(2):
            wt[dest, k] = mm_tn(hp[...], xb[2 * dest + k, 1].reshape(every, wid)).astype(bf16)

    y_far, y_right, y_left = (lax.rem(y + k, ny) for k in (2, 1, 3))

    def y1_copy(way):
        src, dst = wt.at[y_far, way], (yl1 if way else yr1)
        return rdma(src, dst, y_s.at[way], y_r.at[way], d_yl if way else d_yr)

    def y2_copy(way):
        src, dst = wt.at[y_left if way else y_right], (yl2 if way else yr2)
        return rdma(src, dst, y_s.at[2 + way], y_r.at[2 + way], d_yl if way else d_yr)

    def dest_of(k):
        odd = lax.rem(k, 2)
        off = jnp.where(odd == 1, half - (k + 1) // 2, k // 2 - half)
        return lax.rem(z + off + nz, nz)

    def cs_copy(k):
        return rdma(cb.at[k, :, :, 1 - c], sb.at[k], cs_s.at[k], cs_r.at[k], d_sib)

    def x1_copy(k, way):
        dst = (xl1 if way else xr1).at[k]
        return rdma(cb.at[k, way, x_far, c], dst, x1_s.at[way, k], x1_r.at[way, k], d_xl if way else d_xr)

    def x2_copy(k, way):
        src = cb.at[k, :, x_left if way else x_right, c]
        dst = (xl2 if way else xr2).at[k]
        return rdma(src, dst, x2_s.at[way, k], x2_r.at[way, k], d_xl if way else d_xr)

    def zz_copy(way, m, first):
        k = 2 * m if way else jnp.maximum(2 * m - 1, 0)
        src, dst = zs.at[k], (zl_buf if way else zr).at[m]
        if first:
            src, dst = src.at[way], dst.at[way]
        return rdma(src, dst, zz_s.at[way, m], zz_r.at[way, m], d_zl if way else d_zr)

    def zz_wait(way, m):
        @pl.when(m == 0)
        def _():
            zz_copy(way, m, True).wait_recv()

        @pl.when(m > 0)
        def _():
            zz_copy(way, m, False).wait_recv()

    def sum_step(t, carry):
        @pl.when(t < nz)
        def _():
            s = dest_of(t)
            cols = pl.ds(pl.multiple_of(s * wid, wid), wid)
            o = mm(hp[...], wd[:, cols])
            cb[t, 0] = o.astype(bf16).reshape(NX, NC, rows, wid)
            dx = mm(gg[...], wg[:, cols]) + mm(gu[...], wu[:, cols])
            cb[t, 1] = dx.astype(bf16).reshape(NX, NC, rows, wid)
            cs_copy(t).start()

        if ny > 1:

            @pl.when(t == 0)
            def _():
                y_term(y_far)
                for way in range(2):
                    y1_copy(way).start()

        @pl.when((t >= 1) & (t < nz + 1))
        def _():
            k = t - 1
            cs_copy(k).wait_recv()
            cb[k, :, :, c] = (cb[k, :, :, c].astype(f32) + sb[k].astype(f32)).astype(bf16)
            for way in range(2):
                x1_copy(k, way).start()

        if ny > 1:

            @pl.when(t == 1)
            def _():
                y_term(y_right)
                y_term(y_left)

        @pl.when((t >= 2) & (t < nz + 2))
        def _():
            k = t - 2
            for way in range(2):
                x1_copy(k, way).wait_recv()
                to = x_left if way else x_right
                came = (xl1 if way else xr1)[k]
                cb[k, way, to, c] = (cb[k, way, to, c].astype(f32) + came.astype(f32)).astype(bf16)
                x2_copy(k, way).start()

        if ny > 1:

            @pl.when(t == min(4, nz + 2))
            def _():
                for way in range(2):
                    y1_copy(way).wait_recv()
                    to = y_left if way else y_right
                    came = (yl1 if way else yr1)[...]
                    wt[to, way] = (wt[to, way].astype(f32) + came.astype(f32)).astype(bf16)
                    y2_copy(way).start()
                y_term(y)

        @pl.when(t >= 3)
        def _():
            k = t - 3
            for way in range(2):
                x2_copy(k, way).wait_recv()
            got = cb[k, :, x, c].astype(f32) + xr2[k].astype(f32) + xl2[k].astype(f32)
            odd = lax.rem(k, 2)

            @pl.when(k == 0)
            def _():
                zs[0] = got.astype(bf16)
                for way in range(2):
                    zz_copy(way, 0, True).start()

            @pl.when((odd == 1) & (k < nz - 1))
            def _():
                m = (k + 1) // 2
                zz_wait(0, m - 1)
                zs[k] = (got + zr[m - 1].astype(f32)).astype(bf16)
                zz_copy(0, m, False).start()

            @pl.when((odd == 0) & (k > 0))
            def _():
                m = k // 2
                zz_wait(1, m - 1)
                zs[k] = (got + zl_buf[m - 1].astype(f32)).astype(bf16)
                zz_copy(1, m, False).start()

            @pl.when(k == nz - 1)
            def _():
                for way in range(2):
                    zz_copy(way, half - 1, half == 1).wait_recv()
                both = zr[half - 1].astype(f32) + zl_buf[half - 1].astype(f32)
                zs[k] = (got + both).astype(bf16)

        return carry

    lax.fori_loop(0, nz + 3, sum_step, 0)

    for a in range(2):
        final = zs[nz - 1, a]
        stacked = jnp.concatenate(
            [final[:, q * LANES : (q + 1) * LANES] for q in range(q_n)], axis=0
        )
        fp[:, a * packed : (a + 1) * packed, :] = (
            mm(permt[...], stacked).astype(bf16).reshape(nh, packed, LANES)
        )
    f_out = [
        rdma(fp.at[lax.rem(h + k + 1, nh)], hb2.at[k], f_s.at[k], f_r.at[k], dev)
        for k, dev in enumerate(d_h)
    ]
    for cp in f_out:
        cp.start()

    if ny > 1:
        for way in range(2):
            y2_copy(way).wait_recv()
        for k in range(2):
            total = wt[y, k].astype(f32) + yr2[k].astype(f32) + yl2[k].astype(f32)
            gd[:, k * wid : (k + 1) * wid] = total
    else:
        y_term(y)
        for k in range(2):
            gd[:, k * wid : (k + 1) * wid] = wt[y, k].astype(f32)

    for cp in f_out:
        cp.wait_recv()
    total = fp[h].astype(f32)
    for k in range(nh - 1):
        total = total + hb2[k].astype(f32)
    total = total.astype(bf16)
    for a, ref in enumerate((out_m, out_g)):
        tall = mm(spread_p[...], total[a * packed : (a + 1) * packed]).astype(bf16)
        for q in range(q_n):
            ref[:, q * LANES : (q + 1) * LANES] = tall[q * P_ROWS : q * P_ROWS + tok]

    for cp in (*h_out, *f_out):
        cp.wait_send()
    for k in range(3):
        p_copy(k).wait_send()
    p_sib().wait_send()
    if ny > 1:
        for way in range(2):
            y1_copy(way).wait_send()
            y2_copy(way).wait_send()

    def z_drain(d, carry):
        for way in range(2):
            z_copy(way, d, False).wait_send()
        return carry

    def zz_drain(m, carry):
        for way in range(2):
            zz_copy(way, m, False).wait_send()
        return carry

    lax.fori_loop(0, half - 1, z_drain, 0)
    lax.fori_loop(1, half, zz_drain, 0)
    for way in range(2):
        z_copy(way, half - 1, True).wait_send()
        zz_copy(way, 0, True).wait_send()

    def drain(t, carry):
        for way in range(2):
            xa_copy(t, way).wait_send()
            xb_copy(t, way).wait_send()
            x1_copy(t, way).wait_send()
            x2_copy(t, way).wait_send()
        sib_copy(t).wait_send()
        cs_copy(t).wait_send()
        return carry

    lax.fori_loop(0, nz, drain, 0)


def permutations(nh, tok, q_n):
    rows, packed = nh * tok, q_n * tok
    perm = np.zeros((q_n * rows, nh * packed), np.float32)
    permp = np.zeros((rows, nh * P_ROWS), np.float32)
    spread = np.zeros((q_n * P_ROWS, packed), np.float32)
    for q in range(q_n):
        for i in range(tok):
            spread[q * P_ROWS + i, q * tok + i] = 1
    for h in range(nh):
        for i in range(tok):
            permp[h * tok + i, h * P_ROWS + i] = 1
            for q in range(q_n):
                perm[q * rows + h * tok + i, h * packed + q * tok + i] = 1
    return tuple(jnp.asarray(a, bf16) for a in (perm, perm.T, permp, spread, spread.T))


def fused(tokens, grad_out, ids, probs, wg, wu, wd, ny, nh, nz, tok):
    hid, width = wg.shape
    wid = width // nz
    q_n = wid // LANES
    rows = nh * tok
    every = NX * NC * rows
    half = nz // 2
    perms = permutations(nh, tok, q_n)
    vmem, dma = pltpu.VMEM, pltpu.SemaphoreType.DMA
    n_blk = 2 * q_n * tok
    scratch = [
        vmem((n_blk + P_ROWS, LANES), bf16),
        vmem((P_ROWS, wid), bf16),
        vmem((nh, n_blk + P_ROWS, LANES), bf16),
        vmem((NX, NC, rows, LANES), bf16),
        vmem((nz, 2, NX, NC, rows, wid), bf16),
        vmem((hid, width), bf16),
        vmem((hid, width), bf16),
        vmem((hid, width), bf16),
        vmem((every, hid), f32),
        vmem((every, hid), f32),
        vmem((every, hid), f32),
        vmem((every, LANES), f32),
        vmem((every, hid), bf16),
        vmem((every, hid), bf16),
        vmem((every, hid), bf16),
        vmem((nz, 2, NX, NC, rows, wid), bf16),
        vmem((nz, 2, NX, rows, wid), bf16),
        vmem((nz, rows, wid), bf16),
        vmem((nz, rows, wid), bf16),
        vmem((nz, 2, rows, wid), bf16),
        vmem((nz, 2, rows, wid), bf16),
        vmem((nz, 2, rows, wid), bf16),
        vmem((half, 2, rows, wid), bf16),
        vmem((half, 2, rows, wid), bf16),
        vmem((nz // 2, 2, hid, wid), bf16),
        vmem((hid, wid), bf16),
        vmem((hid, wid), bf16),
        vmem((2, hid, wid), bf16),
        vmem((2, hid, wid), bf16),
        vmem((nh, n_blk, LANES), bf16),
        vmem((max(nh - 1, 1), n_blk, LANES), bf16),
        dma((3,)),
        dma((3,)),
        dma((3,)),
        dma((4,)),
        dma((4,)),
        dma((2, half)),
        dma((2, half)),
        dma((2, nz)),
        dma((2, nz)),
        dma((2, nz)),
        dma((2, nz)),
        dma((nz,)),
        dma((nz,)),
        dma((nz,)),
        dma((nz,)),
        dma((2, nz)),
        dma((2, nz)),
        dma((2, nz)),
        dma((2, nz)),
        dma((2, half)),
        dma((2, half)),
        dma((4,)),
        dma((4,)),
        dma((3,)),
        dma((3,)),
    ]
    in_vmem, anywhere = pl.BlockSpec(memory_space=pltpu.VMEM), pl.BlockSpec(memory_space=pl.ANY)
    return pl.pallas_call(
        functools.partial(kernel, ny, nh, nz, tok, wid),
        out_shape=(
            jax.ShapeDtypeStruct((tok, wid), bf16),
            jax.ShapeDtypeStruct((tok, wid), bf16),
            jax.ShapeDtypeStruct((hid, 2 * wid), f32),
        ),
        in_specs=[in_vmem] * 9 + [anywhere] * 3,
        out_specs=(in_vmem, in_vmem, in_vmem),
        scratch_shapes=scratch,
        compiler_params=pltpu.CompilerParams(
            collective_id=0, has_side_effects=True, vmem_limit_bytes=VMEM_BYTES
        ),
        cost_estimate=pl.CostEstimate(
            flops=14 * every * width * hid, bytes_accessed=6 * width * hid, transcendentals=every * hid
        ),
    )(tokens, grad_out, ids, probs, *perms, wg, wu, wd)


def on_device(tokens, grad_out, route_ids, route_probs, w_gate, w_up, w_down):
    tok, wid = tokens.shape
    ny, nz = lax.axis_size("dp"), lax.axis_size("tensor")
    nh = lax.axis_size("expert") // (NX * NC)
    ids, probs = (jnp.pad(a.T, ((0, 0), (0, LANES - tok))) for a in (route_ids, route_probs))
    mixed, grad_tokens, grad_down = fused(
        tokens, grad_out, ids, probs, w_gate[0].T, w_up[0].T, w_down[0], ny, nh, nz, tok
    )
    return (mixed, grad_tokens, grad_down[None])


def solution(mesh):
    return jax.shard_map(
        on_device,
        mesh=mesh,
        in_specs=(
            P(("dp", "expert"), "tensor"),
            P(("dp", "expert"), "tensor"),
            P(("dp", "expert"), None),
            P(("dp", "expert"), None),
            P("expert", None, "tensor"),
            P("expert", None, "tensor"),
            P("expert", "tensor", None),
        ),
        out_specs=(
            P(("dp", "expert"), "tensor"),
            P(("dp", "expert"), "tensor"),
            P("expert", "tensor", "dp"),
        ),
        check_vma=False,
    )
```

```python
import functools

import jax
import jax.numpy as jnp
import numpy as np
from jax import lax
from jax.experimental import pallas as pl
from jax.experimental.pallas import tpu as pltpu
from jax.sharding import PartitionSpec as P

EXPERTS = 32
TOPK = 8
AMAX_TARGET = 4.0
EPS_SCALE = 1e-05
LANES = 128
NX, NC = 4, 2
SLOT = 16
bf16, f32 = jnp.bfloat16, jnp.float32
MESH = pl.DeviceIdType.MESH
VMEM_BYTES = 56 * 1024 * 1024


def mm(a, b):
    return jnp.dot(a, b, preferred_element_type=f32)


def mm_nt(a, b):
    return lax.dot_general(a, b, (((1,), (1,)), ((), ())), preferred_element_type=f32)


def mm_tn(a, b):
    return lax.dot_general(a, b, (((0,), (0,)), ((), ())), preferred_element_type=f32)


def kernel(
    ny, nh, nz, tok, wid,
    tok_in, go_in, ids_in, probs_in, grow_one, shrink_one, wg_h, wu_h, wd_h,
    out_m, out_g, gd,
    pad_in, pb, xb, g4, wg, wu, wd, gate_acc, up_acc, gh_acc, amax, hp, gg, gu,
    cb, sb, xr1, xl1, xr2, xl2, zs, zr, zl_buf, wt, yr1, yl1, yr2, yl2, far,
    w_sem, h_s, h_r, hp_s, hp_r, p_s, p_r, z_s, z_r, xa_s, xa_r, xb_s, xb_r, sib_s, sib_r,
    cs_s, cs_r, x1_s, x1_r, x2_s, x2_r, zz_s, zz_r, y_s, y_r, f_s, f_r,
):
    half = nz // 2
    items = nh * nz
    main = wid - LANES
    groups = main // LANES
    rows = nh * SLOT
    every = NX * NC * rows
    y, e, z = lax.axis_index("dp"), lax.axis_index("expert"), lax.axis_index("tensor")
    c = lax.rem(e, NC)
    x = lax.rem(e // NC, NX)
    h = e // (NC * NX)
    place = h * nz + z

    def eid(h_, x_, c_):
        return (h_ * NX + x_) * NC + c_

    x_right, x_left, x_far = (lax.rem(x + k, NX) for k in (1, 3, 2))
    d_xr, d_xl, d_xf = ((y, eid(h, k, c), z) for k in (x_right, x_left, x_far))
    d_sib = (y, eid(h, x, 1 - c), z)
    d_zr = (y, eid(lax.rem(h + (z + 1) // nz, nh), x, c), lax.rem(z + 1, nz))
    d_zl = (
        y,
        eid(lax.rem(h + nh - 1 + (z + nz - 1) // nz, nh), x, c),
        lax.rem(z + nz - 1, nz),
    )
    jumps = [(0, 1, 3, 2)[r] % nh for r in range(nh)]
    d_h = [(y, eid(lax.rem(h + j, nh), x, c), z) for j in jumps]
    d_yr, d_yl = (lax.rem(y + 1, ny), e, z), (lax.rem(y + ny - 1, ny), e, z)

    def jump(r):
        return jnp.where(r < 2, r, 5 - r)

    def slot(p):
        return pl.ds(pl.multiple_of((p // nz) * SLOT, SLOT), SLOT)

    def rdma(src, dst, s, r, dev):
        return pltpu.make_async_remote_copy(
            src_ref=src, dst_ref=dst, send_sem=s, recv_sem=r, device_id=dev, device_id_type=MESH
        )

    loads = [
        pltpu.make_async_copy(a, b, w_sem.at[i])
        for i, (a, b) in enumerate(((wg_h, wg), (wu_h, wu), (wd_h, wd)))
    ]
    for load in loads:
        load.start()

    partners = [d_xr, d_xl, d_xf, d_sib, d_zr, d_zl, *d_h[1:]]
    if ny > 1:
        partners += [d_yr, d_yl]
    barrier = pltpu.get_barrier_semaphore()
    for dev in partners:
        pl.semaphore_signal(barrier, inc=1, device_id=dev, device_id_type=MESH)

    own = slot(place)
    sub = lax.broadcasted_iota(jnp.int32, (every // SLOT, 8, LANES), 1)
    pad_in[...] = jnp.zeros_like(pad_in)
    for a, ref in enumerate((tok_in, go_in)):
        pad_in[:tok, :] = ref[...]
        for g in range(groups):
            lanes = slice(g * LANES, (g + 1) * LANES)
            moved = mm(shrink_one[g], pad_in[:, main:])
            xb[z, a, x, c, own, lanes] = (pad_in[:, lanes].astype(f32) + moved).astype(bf16)
    expert = lax.broadcasted_iota(jnp.int32, (EXPERTS, LANES), 0)
    dense = jnp.zeros((EXPERTS, LANES), f32)
    for k in range(TOPK):
        dense = dense + jnp.where(expert == ids_in[k : k + 1, :], probs_in[k : k + 1, :], 0.0)
    high = dense.astype(bf16).astype(f32)
    middle = (dense - high).astype(bf16).astype(f32)
    tall = jnp.concatenate([high, middle, dense - high - middle, jnp.zeros_like(dense)], axis=0)
    pb[x, c, own] = tall.T[:SLOT].astype(bf16)
    gate_acc[...] = jnp.zeros_like(gate_acc)
    up_acc[...] = jnp.zeros_like(up_acc)
    gh_acc[...] = jnp.zeros_like(gh_acc)
    amax[...] = jnp.zeros_like(amax)
    zr[0, 1] = jnp.zeros_like(zr[0, 1])
    zl_buf[0, 0] = jnp.zeros_like(zl_buf[0, 0])
    pl.semaphore_wait(barrier, len(partners))

    back = [jumps.index((nh - j) % nh) for j in jumps]
    h_out = [
        rdma(xb.at[z, :, x, c, own], xb.at[z, :, x, c, own], h_s.at[r], h_r.at[back[r]], d_h[r])
        for r in range(1, nh)
    ]
    hp_out = [
        rdma(pb.at[x, c, own], pb.at[x, c, own], hp_s.at[r], hp_r.at[r], d_h[r])
        for r in range(1, nh)
    ]
    for cp, cp_p in zip(h_out, hp_out):
        cp.start()
        cp_p.start()

    others = max(nh - 1, 1)

    def turn(u):
        w = jnp.maximum(u - nz, 0)
        first = u < nz
        return jnp.where(first, 0, 1 + lax.rem(w, others)), jnp.where(first, u, w // others)

    def source(u):
        r, t = turn(u)
        d = (t + 1) // 2
        return lax.rem(place + d * (1 - 2 * lax.rem(t, 2)) + nz * jump(r) + items, items)

    def z_copy(way, r, d):
        p = lax.rem(place + (d if way else -d) + nz * jump(r) + items, items)
        ref = xb.at[lax.rem(p, nz), :, x, c, slot(p)]
        i = r * half + d
        return rdma(ref, ref, z_s.at[way, i], z_r.at[way, i], d_zl if way else d_zr)

    def xa_copy(u, way):
        p = source(u)
        ref = xb.at[lax.rem(p, nz), :, x, c, slot(p)]
        return rdma(ref, ref, xa_s.at[way, u], xa_r.at[way, u], d_xl if way else d_xr)

    def xb_copy(u, way):
        p = source(u)
        ref = xb.at[lax.rem(p, nz), :, x_right if way else x_left, c, slot(p)]
        return rdma(ref, ref, xb_s.at[u], xb_r.at[u], d_xl if way else d_xr)

    def sib_copy(u):
        p = source(u)
        ref = xb.at[lax.rem(p, nz), :, :, c, slot(p)]
        return rdma(ref, ref, sib_s.at[u], sib_r.at[u], d_sib)

    def p_copy(k):
        ref = pb.at[x, c]
        return rdma(ref, ref, p_s.at[k], p_r.at[k], (d_xr, d_xl, d_xf)[k])

    def p_sib():
        ref = pb.at[:, c]
        return rdma(ref, ref, p_s.at[3], p_r.at[3], d_sib)

    p_at = items - 8 if items > 8 else 0
    lag_a, lag_b, lag_c = 4, 7, 9

    def gather_step(v, carry):
        @pl.when(v < items)
        def _():
            r, t = turn(v)
            d = (t + 1) // 2
            odd = lax.rem(t, 2)
            for k in range(1, nh):

                @pl.when(v == nz + k - 1)
                def _():
                    h_out[back[k] - 1].wait_recv()

            @pl.when((t > 0) & (odd == 1))
            def _():
                z_copy(0, r, d - 1).wait_recv()

            @pl.when((t > 0) & (odd == 0))
            def _():
                z_copy(1, r, d - 1).wait_recv()

            @pl.when(((t == 0) | (odd == 1)) & (d < half))
            def _():
                z_copy(0, r, d).start()

            @pl.when((odd == 0) & (d < half - 1))
            def _():
                z_copy(1, r, d).start()

            for way in range(2):
                xa_copy(v, way).start()

            @pl.when(v == p_at)
            def _():
                for cp in hp_out:
                    cp.wait_recv()
                for k in range(3):
                    p_copy(k).start()

        @pl.when((v >= lag_a) & (v < items + lag_a))
        def _():
            u = v - lag_a
            for way in range(2):
                xa_copy(u, way).wait_recv()

                @pl.when(lax.rem(u, 2) == way)
                def _():
                    xb_copy(u, way).start()

        @pl.when((v >= lag_b) & (v < items + lag_b))
        def _():
            u = v - lag_b
            xb_copy(u, 0).wait_recv()
            sib_copy(u).start()

            @pl.when(u == p_at)
            def _():
                for k in range(3):
                    p_copy(k).wait_recv()
                p_sib().start()

        @pl.when(v == 3)
        def _():
            for load in loads:
                load.wait()

        @pl.when(v >= lag_c)
        def _():
            sib_copy(v - lag_c).wait_recv()

        @pl.when((v - lag_c >= (nz if nh > 1 else 0)) & (turn(jnp.maximum(v - lag_c, 0))[0] == nh - 1))
        def _():
            s = lax.rem(source(v - lag_c), nz)
            cols = pl.ds(pl.multiple_of(s * wid, wid), wid)

            def whole(a):
                part = xb[s, a].reshape(every, main)
                end = part.astype(f32).reshape(every // SLOT, SLOT, main)[:, 8:]
                first, second, third = (end[..., g * LANES : (g + 1) * LANES] for g in range(groups))
                upper = jnp.where(sub < 4, pltpu.roll(first, 4, 1), second)
                lower = jnp.where(sub < 4, pltpu.roll(third, 4, 1), 0.0)
                rest = jnp.concatenate([upper, lower], axis=1).reshape(every, LANES)
                return part, rest.astype(bf16)

            x_part, x_rest = whole(0)
            x_rows = jnp.concatenate([x_part, x_rest], axis=1)
            gate_acc[...] += mm_nt(x_rows, wg[:, cols])
            up_acc[...] += mm_nt(x_rows, wu[:, cols])
            g_part, g_rest = whole(1)
            g4[s] = g_rest
            gh_acc[...] += mm_nt(jnp.concatenate([g_part, g_rest], axis=1), wd[:, cols])
            size = jnp.abs(x_rows.astype(f32))
            top = amax[...]
            for q in range(groups + 1):
                top = jnp.maximum(top, size[:, q * LANES : (q + 1) * LANES])
            amax[...] = top

        return carry

    lax.fori_loop(0, items + lag_c, gather_step, 0)

    p_sib().wait_recv()
    lane = lax.broadcasted_iota(jnp.int32, (every, LANES), 1)
    mine = (lane == e) | (lane == e + EXPERTS) | (lane == e + 2 * EXPERTS)
    prob = jnp.sum(
        jnp.where(mine, pb[...].reshape(every, LANES).astype(f32), 0.0), axis=1, keepdims=True
    )
    factor = AMAX_TARGET / (jnp.max(amax[...], axis=1, keepdims=True) + EPS_SCALE)
    gate = gate_acc[...] * factor
    upval = up_acc[...] * factor
    sigma = jax.nn.sigmoid(gate)
    active = gate * sigma
    grad = gh_acc[...] * (prob * factor)
    hp[...] = (prob * active * upval).astype(bf16)
    gg[...] = (grad * upval * sigma * (1.0 + gate * (1.0 - sigma))).astype(bf16)
    gu[...] = (grad * active).astype(bf16)

    def y_term(dest):
        for k in range(2):
            s = 2 * dest + k
            wt[dest, k, :, :main] = mm_tn(hp[...], xb[s, 1].reshape(every, main)).astype(bf16)
            wt[dest, k, :, main:] = mm_tn(hp[...], g4[s]).astype(bf16)

    y_far, y_right, y_left = (lax.rem(y + k, ny) for k in (2, 1, 3))

    def y1_copy(way):
        src, dst = wt.at[y_far, way], (yl1 if way else yr1)
        return rdma(src, dst, y_s.at[way], y_r.at[way], d_yl if way else d_yr)

    def y2_copy(way):
        src, dst = wt.at[y_left if way else y_right], (yl2 if way else yr2)
        return rdma(src, dst, y_s.at[2 + way], y_r.at[2 + way], d_yl if way else d_yr)

    def dest_of(k):
        odd = lax.rem(k, 2)
        off = jnp.where(odd == 1, half - (k + 1) // 2, k // 2 - half)
        return lax.rem(z + off + nz, nz)

    def cs_copy(k):
        return rdma(cb.at[k, :, :, 1 - c], sb.at[k], cs_s.at[k], cs_r.at[k], d_sib)

    def x1_copy(k, way):
        dst = (xl1 if way else xr1).at[k]
        return rdma(cb.at[k, way, x_far, c], dst, x1_s.at[way, k], x1_r.at[way, k], d_xl if way else d_xr)

    def x2_copy(k, way):
        src = cb.at[k, :, x_left if way else x_right, c]
        dst = (xl2 if way else xr2).at[k]
        return rdma(src, dst, x2_s.at[way, k], x2_r.at[way, k], d_xl if way else d_xr)

    def zz_copy(way, m, first):
        k = 2 * m if way else jnp.maximum(2 * m - 1, 0)
        src, dst = zs.at[k], (zl_buf if way else zr).at[m]
        if first:
            src, dst = src.at[way], dst.at[way]
        return rdma(src, dst, zz_s.at[way, m], zz_r.at[way, m], d_zl if way else d_zr)

    def zz_wait(way, m):
        @pl.when(m == 0)
        def _():
            zz_copy(way, m, True).wait_recv()

        @pl.when(m > 0)
        def _():
            zz_copy(way, m, False).wait_recv()

    def packed(value):
        last = value[:, main:].reshape(every // SLOT, SLOT, LANES)
        moved = (pltpu.roll(last[:, :8], 4, 1), last[:, :8], pltpu.roll(last[:, 8:], 4, 1))
        parts = []
        for g in range(groups):
            lanes = value[:, g * LANES : (g + 1) * LANES].reshape(every // SLOT, SLOT, LANES)
            lower = jnp.where(sub < 4, lanes[:, 8:], moved[g])
            parts.append(jnp.concatenate([lanes[:, :8], lower], axis=1).reshape(every, LANES).astype(bf16))
        return jnp.concatenate(parts, axis=1).reshape(NX, NC, rows, main)

    def sum_step(t, carry):
        @pl.when(t < nz)
        def _():
            s = dest_of(t)
            cols = pl.ds(pl.multiple_of(s * wid, wid), wid)
            cb[t, 0] = packed(mm(hp[...], wd[:, cols]))
            cb[t, 1] = packed(mm(gg[...], wg[:, cols]) + mm(gu[...], wu[:, cols]))
            cs_copy(t).start()

        if ny > 1:

            @pl.when(t == 0)
            def _():
                y_term(y_far)
                for way in range(2):
                    y1_copy(way).start()

        @pl.when((t >= 1) & (t < nz + 1))
        def _():
            k = t - 1
            cs_copy(k).wait_recv()
            cb[k, :, :, c] = (cb[k, :, :, c].astype(f32) + sb[k].astype(f32)).astype(bf16)
            for way in range(2):
                x1_copy(k, way).start()

        if ny > 1:

            @pl.when(t == 1)
            def _():
                y_term(y_right)
                y_term(y_left)

        @pl.when((t >= 2) & (t < nz + 2))
        def _():
            k = t - 2
            for way in range(2):
                x1_copy(k, way).wait_recv()
                to = x_left if way else x_right
                came = (xl1 if way else xr1)[k]
                cb[k, way, to, c] = (cb[k, way, to, c].astype(f32) + came.astype(f32)).astype(bf16)
                x2_copy(k, way).start()

        if ny > 1:

            @pl.when(t == min(4, nz + 2))
            def _():
                for way in range(2):
                    y1_copy(way).wait_recv()
                    to = y_left if way else y_right
                    came = (yl1 if way else yr1)[...]
                    wt[to, way] = (wt[to, way].astype(f32) + came.astype(f32)).astype(bf16)
                    y2_copy(way).start()
                y_term(y)

        @pl.when(t >= 3)
        def _():
            k = t - 3
            for way in range(2):
                x2_copy(k, way).wait_recv()
            got = cb[k, :, x, c].astype(f32) + xr2[k].astype(f32) + xl2[k].astype(f32)
            odd = lax.rem(k, 2)

            @pl.when(k == 0)
            def _():
                zs[0] = got.astype(bf16)
                for way in range(2):
                    zz_copy(way, 0, True).start()

            @pl.when((odd == 1) & (k < nz - 1))
            def _():
                m = (k + 1) // 2
                zz_wait(0, m - 1)
                zs[k] = (got + zr[m - 1].astype(f32)).astype(bf16)
                zz_copy(0, m, False).start()

            @pl.when((odd == 0) & (k > 0))
            def _():
                m = k // 2
                zz_wait(1, m - 1)
                zs[k] = (got + zl_buf[m - 1].astype(f32)).astype(bf16)
                zz_copy(1, m, False).start()

            @pl.when(k == nz - 1)
            def _():
                for way in range(2):
                    zz_copy(way, half - 1, half == 1).wait_recv()
                both = zr[half - 1].astype(f32) + zl_buf[half - 1].astype(f32)
                zs[k] = (got + both).astype(bf16)

        return carry

    lax.fori_loop(0, nz + 3, sum_step, 0)

    def f_copy(r):
        src = zs.at[nz - 1, :, slot(lax.rem(place + nz * jumps[r], items))]
        return rdma(src, far.at[r - 1], f_s.at[r], f_r.at[r], d_h[r])

    for r in range(1, nh):
        f_copy(r).start()

    if ny > 1:
        for way in range(2):
            y2_copy(way).wait_recv()
        for k in range(2):
            total = wt[y, k].astype(f32) + yr2[k].astype(f32) + yl2[k].astype(f32)
            gd[:, k * wid : (k + 1) * wid] = total
    else:
        y_term(y)
        for k in range(2):
            gd[:, k * wid : (k + 1) * wid] = wt[y, k].astype(f32)

    for r in range(1, nh):
        f_copy(r).wait_recv()
    total = zs[nz - 1, :, own].astype(f32)
    for r in range(nh - 1):
        total = total + far[r].astype(f32)
    total = total.astype(bf16)
    for a, ref in enumerate((out_m, out_g)):
        last = jnp.zeros((SLOT, LANES), f32)
        for g in range(groups):
            lanes = total[a][:, g * LANES : (g + 1) * LANES]
            ref[:, g * LANES : (g + 1) * LANES] = lanes[:tok]
            last = last + mm(grow_one[g], lanes)
        ref[:, main:] = last[:tok].astype(bf16)

    for cp in (*h_out, *hp_out):
        cp.wait_send()
    for k in range(3):
        p_copy(k).wait_send()
    p_sib().wait_send()
    for r in range(1, nh):
        f_copy(r).wait_send()
    if ny > 1:
        for way in range(2):
            y1_copy(way).wait_send()
            y2_copy(way).wait_send()

    def z_drain(r, carry):
        for d in range(half):
            z_copy(0, r, d).wait_send()
        for d in range(half - 1):
            z_copy(1, r, d).wait_send()
        return carry

    for way in range(2):
        zz_copy(way, 0, True).wait_send()
        for m in range(1, half):
            zz_copy(way, m, False).wait_send()

    def sum_drain(k, carry):
        for way in range(2):
            x1_copy(k, way).wait_send()
            x2_copy(k, way).wait_send()
        cs_copy(k).wait_send()
        return carry

    lax.fori_loop(0, nz, sum_drain, 0)

    def drain(u, carry):
        for way in range(2):
            xa_copy(u, way).wait_send()
        xb_copy(u, 0).wait_send()
        sib_copy(u).wait_send()
        return carry

    lax.fori_loop(0, nh, z_drain, 0)
    lax.fori_loop(0, items, drain, 0)


def selections(tok, groups):
    one = np.zeros((groups, SLOT, SLOT), np.float32)
    for i in range(tok):
        one[i // 4, i, tok + i % 4] = 1
    return tuple(jnp.asarray(a, bf16) for a in (one, one.transpose(0, 2, 1)))


def fused(tokens, grad_out, ids, probs, wg, wu, wd, ny, nh, nz, tok):
    hid, width = wg.shape
    wid = width // nz
    main = wid - LANES
    rows = nh * SLOT
    every = NX * NC * rows
    half = nz // 2
    items = nh * nz
    vmem, dma = pltpu.VMEM, pltpu.SemaphoreType.DMA
    block = (2, SLOT, main)
    scratch = [
        vmem((SLOT, wid), bf16),
        vmem((NX, NC, rows, LANES), bf16),
        vmem((nz, 2, NX, NC, rows, main), bf16),
        vmem((nz, every, LANES), bf16),
        vmem((hid, width), bf16),
        vmem((hid, width), bf16),
        vmem((hid, width), bf16),
        vmem((every, hid), f32),
        vmem((every, hid), f32),
        vmem((every, hid), f32),
        vmem((every, LANES), f32),
        vmem((every, hid), bf16),
        vmem((every, hid), bf16),
        vmem((every, hid), bf16),
        vmem((nz, 2, NX, NC, rows, main), bf16),
        vmem((nz, 2, NX, rows, main), bf16),
        vmem((nz, rows, main), bf16),
        vmem((nz, rows, main), bf16),
        vmem((nz, 2, rows, main), bf16),
        vmem((nz, 2, rows, main), bf16),
        vmem((nz, 2, rows, main), bf16),
        vmem((half, 2, rows, main), bf16),
        vmem((half, 2, rows, main), bf16),
        vmem((nz // 2, 2, hid, wid), bf16),
        vmem((hid, wid), bf16),
        vmem((hid, wid), bf16),
        vmem((2, hid, wid), bf16),
        vmem((2, hid, wid), bf16),
        vmem((max(nh - 1, 1), *block), bf16),
        dma((3,)),
        *[dma((nh,))] * 4,
        *[dma((4,))] * 2,
        *[dma((2, nh * half))] * 2,
        *[dma((2, items))] * 2,
        *[dma((items,))] * 2,
        *[dma((items,))] * 2,
        *[dma((nz,))] * 2,
        *[dma((2, nz))] * 2,
        *[dma((2, nz))] * 2,
        *[dma((2, half))] * 2,
        *[dma((4,))] * 2,
        *[dma((nh,))] * 2,
    ]
    in_vmem, anywhere = pl.BlockSpec(memory_space=pltpu.VMEM), pl.BlockSpec(memory_space=pl.ANY)
    return pl.pallas_call(
        functools.partial(kernel, ny, nh, nz, tok, wid),
        out_shape=(
            jax.ShapeDtypeStruct((tok, wid), bf16),
            jax.ShapeDtypeStruct((tok, wid), bf16),
            jax.ShapeDtypeStruct((hid, 2 * wid), f32),
        ),
        in_specs=[in_vmem] * 6 + [anywhere] * 3,
        out_specs=(in_vmem, in_vmem, in_vmem),
        scratch_shapes=scratch,
        compiler_params=pltpu.CompilerParams(
            collective_id=0, has_side_effects=True, vmem_limit_bytes=VMEM_BYTES
        ),
        cost_estimate=pl.CostEstimate(
            flops=14 * every * width * hid, bytes_accessed=6 * width * hid, transcendentals=every * hid
        ),
    )(tokens, grad_out, ids, probs, *selections(tok, main // LANES), wg, wu, wd)


def on_device(tokens, grad_out, route_ids, route_probs, w_gate, w_up, w_down):
    tok, wid = tokens.shape
    ny, nz = lax.axis_size("dp"), lax.axis_size("tensor")
    nh = lax.axis_size("expert") // (NX * NC)
    ids, probs = (jnp.pad(a.T, ((0, 0), (0, LANES - tok))) for a in (route_ids, route_probs))
    mixed, grad_tokens, grad_down = fused(
        tokens, grad_out, ids, probs, w_gate[0].T, w_up[0].T, w_down[0], ny, nh, nz, tok
    )
    return (mixed, grad_tokens, grad_down[None])


def solution(mesh):
    return jax.shard_map(
        on_device,
        mesh=mesh,
        in_specs=(
            P(("dp", "expert"), "tensor"),
            P(("dp", "expert"), "tensor"),
            P(("dp", "expert"), None),
            P(("dp", "expert"), None),
            P("expert", None, "tensor"),
            P("expert", None, "tensor"),
            P("expert", "tensor", None),
        ),
        out_specs=(
            P(("dp", "expert"), "tensor"),
            P(("dp", "expert"), "tensor"),
            P("expert", "tensor", "dp"),
        ),
        check_vma=False,
    )
```
